512 devices in a mesh: tm: 64 (over z, y_hi, core), tile: 8 (over x, y_lo).
Axes of the slice: x: 4, y: 8 (y_hi: 4, y_lo: 2; y = y_hi * 2 + y_lo), z: 8, core: 2. Of those that a mesh axis runs over, the one named last changes fastest.
Arguments:
- frames: bfloat16 [32768, 512], P('tm'), may hold values from -6 to 6
- freq: bfloat16 [512, 8192], P(None, 'tile'), may hold values from -0.25 to 0.25
- phase: bfloat16 [8192], P('tile'), may hold values from -3.140625 to 3.140625
- seg_end: int32 [32768], P('tm'), may hold values from 0 to 32767, as said below
Outputs:
- panel_factor: float32 [8192, 1024], P(('tile', 'tm'))
- lag_scores: float32 [1024, 8192], P(None, ('tile', 'tm'))
The draws below stay inside these ranges and needn't reach their ends.
Inputs may be any that keep to these rules, and one draw needn't show every extreme that they name: seg_end never falls, seg_end[t] >= t, and it is constant within a segment: a segment runs from the frame after the previous segment's end to its seg_end; the last segment ends at 32767.
All inputs are finite; a program needn't handle non-finite values.
Results may differ from the reference program's by a relative error of at most 0.00098.
Values may be sent and summed in bfloat16 or wider, within the bound.
No kernel may reach another device: no remote copies, remote signals or barrier semaphores. Data moves between devices by JAX's collectives and lax.ppermute only.
A program may use at most 128 MiB of HBM per device.

```python
import jax
import jax.numpy as jnp
from jax import lax

DIN = 512
M = 8192
P_SIZE = 1024
LAG = 96
F_DEV = 512
FRAMES = 32768
N_TM = 64


def draw_seg_end(key, part):
    key = jax.random.fold_in(key, 7)
    where_at = jnp.arange(FRAMES, dtype=jnp.int32)
    starts = jax.random.randint(key, (FRAMES,), 0, 2 * F_DEV) == 0
    starts = jnp.logical_or(starts, where_at == 0)
    start_pos = jnp.where(starts, where_at, FRAMES).astype(jnp.int32)
    later = jnp.concatenate([start_pos[1:], jnp.full((1,), FRAMES, jnp.int32)])
    return (lax.cummin(later, reverse=True) - 1).astype(jnp.int32)


def block_scale(rng, extent, cuts, least, high):
    loudness = 1.0
    for dim, blocks in cuts:
        heights = jax.random.uniform(jax.random.fold_in(jax.random.fold_in(rng, 6), dim), (blocks,), jnp.float32, least / len(cuts), high / len(cuts))
        loudness = loudness * jnp.repeat(jnp.exp(heights), extent[dim] // blocks).reshape((-1,) + (1,) * (len(extent) - 1 - dim))
    return loudness


def noise(stream_key, dims, deviation, reach, cuts=(), held_as=jnp.bfloat16):
    loudness = block_scale(stream_key, dims, cuts, -0.22, 0.18) if cuts else 1.0
    array = jax.random.normal(stream_key, dims, jnp.float32) * deviation * loudness
    return jnp.minimum(jnp.maximum(array, -reach), reach).astype(held_as)


def setup_inputs(seed: int = 0) -> dict:
    seeds = jax.random.split(jax.random.key(seed), 5)
    return {
        "frames": noise(seeds[0], (FRAMES, DIN), 1.0, 6.0, ((0, 64),)),
        "freq": noise(seeds[1], (DIN, M), DIN ** -0.5, 0.25, ((1, 8),)),
        "phase": jnp.clip(jax.random.uniform(seeds[2], (M,), jnp.float32, -3.140625, 3.140625), -3.140625, 3.140625).astype(jnp.bfloat16),
        "seg_end": draw_seg_end(jax.random.fold_in(seeds[4], 71), 0),
    }


ridge = 0.05

def lift_rows(rows, freq, phase):
    angle = jnp.dot(rows.astype(jnp.float32), freq.astype(jnp.float32), preferred_element_type=jnp.float32) + phase.astype(jnp.float32)
    return jnp.cos(angle).astype(jnp.bfloat16)

def reference(frames, freq, phase, seg_end):
    padded = jnp.concatenate([frames, jnp.zeros((LAG, DIN), jnp.bfloat16)], axis=0)

    def step(carry, start):
        gram_acc, cross_acc = carry
        rows = lax.dynamic_slice(padded, (start, jnp.int32(0)), (F_DEV + LAG, DIN))
        feats = lift_rows(rows, freq, phase)
        first = feats[:F_DEV]
        second = feats[LAG:]
        ends = lax.dynamic_slice(seg_end, (start,), (F_DEV,))
        where_at = start + jnp.arange(F_DEV, dtype=jnp.int32)
        valid = (where_at + LAG <= ends).astype(jnp.bfloat16)[:, None]
        masked = first[:, :P_SIZE] * valid
        gram_acc = gram_acc + jnp.dot(first.T.astype(jnp.float32), masked.astype(jnp.float32), preferred_element_type=jnp.float32)
        cross_acc = cross_acc + jnp.dot(masked.T.astype(jnp.float32), second.astype(jnp.float32), preferred_element_type=jnp.float32)
        return ((gram_acc, cross_acc), None)
    starts = jnp.arange(N_TM, dtype=jnp.int32) * F_DEV
    init = (jnp.zeros((M, P_SIZE), jnp.float32), jnp.zeros((P_SIZE, M), jnp.float32))
    (gram, cross), _ = lax.scan(step, init, starts)
    gram = gram / FRAMES + ridge * jnp.eye(M, P_SIZE, dtype=jnp.float32)
    cross = cross / FRAMES
    chol = jnp.linalg.cholesky(gram[:P_SIZE])
    panel_factor = jax.scipy.linalg.solve_triangular(chol, gram.T, lower=True).T
    lag_scores = jnp.sqrt(jnp.float32(FRAMES)) * jax.scipy.linalg.solve_triangular(chol, cross, lower=True)
    return (panel_factor, lag_scores)
```

```python
import jax
import jax.numpy as jnp
from jax import lax
from jax.experimental import pallas as pl
from jax.experimental.pallas import tpu as pltpu
from jax.sharding import Mesh, PartitionSpec as P

PANEL = 1024
LAG = 96
BLOCK = 128
GROUP = 16
RIDGE = 0.05
FRAMES = 32768

F32 = jnp.float32
BF16 = jnp.bfloat16

COSINE = (
    1.0,
    -19.73920440673828,
    64.93911743164062,
    -85.45016479492188,
    60.16783142089844,
    -25.968313217163086,
    6.529610633850098,
)


def cosine(angle):
    turns = angle * F32(0.15915494309189535)
    turns = turns - jnp.round(turns)
    square = turns * turns
    value = jnp.full_like(square, COSINE[-1])
    for factor in COSINE[-2::-1]:
        value = value * square + F32(factor)
    return value


def lift_rows(rows, freq, phase):
    angle = jnp.dot(rows, freq, preferred_element_type=F32) + phase.astype(F32)
    return cosine(angle).astype(BF16)


def over_frames(left, right):
    return lax.dot_general(left, right, (((0,), (0,)), ((), ())), preferred_element_type=F32)


def swap(value):
    return lax.ppermute(value, "c", [(0, 1), (1, 0)])


def gather(value, axes):
    count = 1
    for axis in axes:
        count *= lax.axis_size(axis)
    copies = jnp.broadcast_to(value[None], (count,) + value.shape)
    return lax.all_to_all(copies, axes, 0, 0, tiled=True)


def product(left, right, dims=((1,), (0,))):
    return lax.dot_general(
        left, right, (dims, ((), ())), precision=lax.Precision.HIGHEST, preferred_element_type=F32
    )


def reciprocal(value):
    guess = pl.reciprocal(value, approx=True)
    return guess * (2.0 - value * guess)


def inverse_factor(block):
    row = lax.broadcasted_iota(jnp.int32, (BLOCK, BLOCK), 0)
    col = lax.broadcasted_iota(jnp.int32, (BLOCK, BLOCK), 1)
    eye = (row == col).astype(F32)
    rows = lax.broadcasted_iota(jnp.int32, (GROUP, BLOCK), 0)
    left, right = [], []
    for lo in range(0, BLOCK, GROUP):
        s, t = block[lo : lo + GROUP], eye[lo : lo + GROUP]
        if lo:
            above = jnp.concatenate(left, axis=0)
            beside = jnp.concatenate(right, axis=0)
            done = product(
                above[:, lo : lo + GROUP], jnp.concatenate([above, beside], axis=1), ((0,), (0,))
            )
            s, t = s - done[:, :BLOCK], t - done[:, BLOCK:]
        cols = [jnp.broadcast_to(s[:, lo + k : lo + k + 1], (GROUP, BLOCK)) for k in range(GROUP)]
        diag = jnp.ones((GROUP, BLOCK), F32)
        for j in range(GROUP):
            pivot = cols[j][j : j + 1]
            diag = jnp.where(rows == j, pivot, diag)
            if j < GROUP - 1:
                ratio = jnp.where(rows > j, cols[j] * reciprocal(pivot), 0.0)
                for k in range(j + 1, GROUP):
                    cols[k] = cols[k] - ratio * cols[k][j : j + 1]
                s, t = s - ratio * s[j : j + 1], t - ratio * t[j : j + 1]
        scale = lax.rsqrt(diag)
        left.append(s * scale)
        right.append(t * scale)
    return jnp.concatenate(right, axis=0)


def factor_kernel(packed_ref, next_ref, inverse_ref, a_ref):
    blocks = PANEL // BLOCK
    row = lax.broadcasted_iota(jnp.int32, (BLOCK, BLOCK), 0)
    col = lax.broadcasted_iota(jnp.int32, (BLOCK, BLOCK), 1)
    ridge = jnp.where(row == col, F32(RIDGE), F32(0.0))
    for i in range(blocks):
        lo = i * BLOCK
        if i < blocks // 2:
            part = packed_ref[i, :, : PANEL - lo]
        else:
            part = packed_ref[blocks - 1 - i, :, lo + BLOCK :]
        a_ref[lo : lo + BLOCK, lo:] = part * F32(1.0 / FRAMES)
        a_ref[lo : lo + BLOCK, lo : lo + BLOCK] = a_ref[lo : lo + BLOCK, lo : lo + BLOCK] + ridge
    for p in range(blocks):
        lo = p * BLOCK
        hi = lo + BLOCK
        inverse = inverse_factor(a_ref[lo:hi, lo:hi])
        inverse_ref[p] = inverse
        if p + 1 < blocks:
            upper = product(inverse, a_ref[lo:hi, hi:])
            for k in range(hi, PANEL, BLOCK):
                a_ref[k : k + BLOCK, k:] = a_ref[k : k + BLOCK, k:] - product(
                    upper[:, k - hi : k - hi + BLOCK], upper[:, k - hi :], ((0,), (0,))
                )
            next_ref[lo:hi, hi:] = product(inverse, upper, ((0,), (0,)))


def factor(packed):
    out = jax.ShapeDtypeStruct
    in_vmem = pl.BlockSpec(memory_space=pltpu.VMEM)
    return pl.pallas_call(
        factor_kernel,
        out_shape=(
            out((PANEL, PANEL), F32),
            out((PANEL // BLOCK, BLOCK, BLOCK), F32),
        ),
        in_specs=[in_vmem],
        out_specs=(in_vmem, in_vmem),
        scratch_shapes=[pltpu.VMEM((PANEL, PANEL), F32)],
        compiler_params=pltpu.CompilerParams(vmem_limit_bytes=40 << 20),
        cost_estimate=pl.CostEstimate(
            flops=45_000_000_000, bytes_accessed=10_000_000, transcendentals=0
        ),
        name="factor",
    )(packed)


def solve_kernel(rows_ref, next_ref, inverse_ref, out_ref):
    rest = rows_ref[...]
    for p in range(PANEL // BLOCK):
        lo = p * BLOCK
        head = rest[:, :BLOCK]
        out_ref[:, lo : lo + BLOCK] = product(head, inverse_ref[p], ((1,), (1,)))
        if lo + BLOCK < PANEL:
            rest = rest[:, BLOCK:] - product(head, next_ref[lo : lo + BLOCK, lo + BLOCK :])


def solve(rows, right, inverse):
    in_vmem = pl.BlockSpec(memory_space=pltpu.VMEM)
    return pl.pallas_call(
        solve_kernel,
        out_shape=jax.ShapeDtypeStruct(rows.shape, F32),
        in_specs=[in_vmem] * 3,
        out_specs=in_vmem,
        compiler_params=pltpu.CompilerParams(vmem_limit_bytes=40 << 20),
        cost_estimate=pl.CostEstimate(
            flops=4_000_000_000, bytes_accessed=5_000_000, transcendentals=0
        ),
        name="solve",
    )(rows, right, inverse)


def per_device(frames, freq, phase, seg_end):
    n_z, n_yh, n_c = (lax.axis_size(a) for a in ("z", "yh", "c"))
    n_pair = n_z * n_yh
    n_tm = n_pair * n_c
    f_dev, din = frames.shape
    block = freq.shape[1]
    width = block // n_tm
    c = lax.axis_index("c")
    x = lax.axis_index("x")
    yl = lax.axis_index("yl")
    pair = lax.axis_index("z") * n_yh + lax.axis_index("yh")
    tm = pair * n_c + c
    tile = x * lax.axis_size("yl") + yl

    half = din // n_c
    mine = lax.dynamic_slice(freq, (c * half, 0), (half, block))
    chunks = jnp.concatenate(
        [mine.reshape(8, half // 8, block), jnp.broadcast_to(phase[None, None], (8, 1, block))],
        axis=1,
    )
    chunk = lax.all_to_all(chunks, ("x", "yl"), 0, 0, tiled=True)[0]
    halves = gather(chunk, ("x", "yl"))
    panel_phase = halves[0, half // 8]
    mine = halves[:, : half // 8].reshape(half, block)
    other = swap(mine)
    panel_freq = jnp.where(
        c == 0, jnp.concatenate([mine, other]), jnp.concatenate([other, mine])
    )

    where_at = tm * f_dev + jnp.arange(f_dev, dtype=jnp.int32)
    valid = (where_at + LAG <= seg_end).astype(BF16)
    head = lax.ppermute(
        frames[:LAG], ("z", "yh", "c"), [(source, source - 1) for source in range(1, n_tm)]
    )
    extended = jnp.concatenate([frames, head, valid.reshape(f_dev // din, din)], axis=0)
    sibling = swap(extended)
    first = jnp.where(c == 0, extended, sibling)
    second = jnp.where(c == 0, sibling, extended)
    rows = jnp.concatenate([first[:f_dev], second[: f_dev + LAG]], axis=0)
    both_valid = jnp.concatenate([first[f_dev + LAG :], second[f_dev + LAG :]]).reshape(-1, 1)
    n_rows = 2 * f_dev

    column = jnp.arange(block // n_c, dtype=jnp.int32)
    source = (column // width) * (n_c * width) + c * width + column % width
    pick = (jnp.arange(block, dtype=jnp.int32)[:, None] == source[None, :]).astype(BF16)
    own_freq = jnp.dot(freq, pick, preferred_element_type=F32).astype(BF16)
    own_phase = jnp.dot(phase[None], pick, preferred_element_type=F32)[0]

    panel = lift_rows(rows[:n_rows], panel_freq, panel_phase)
    masked = panel * both_valid
    lifted = lift_rows(rows, own_freq, own_phase)

    quarter = yl * n_c + c
    n_block = PANEL // BLOCK
    rows_x = lax.dynamic_slice(panel, (0, x * BLOCK + quarter * 32), (n_rows, 32))
    rows_y = lax.dynamic_slice(panel, (0, (n_block - 1 - x) * BLOCK + quarter * 32), (n_rows, 32))
    both = over_frames(jnp.concatenate([rows_x, rows_y], axis=1), masked)
    padded = jnp.pad(both[:32], ((0, 0), (0, BLOCK * n_block // 2)))
    upper_x = lax.dynamic_slice(padded, (0, x * BLOCK), (32, PANEL))
    place = jnp.arange(PANEL + BLOCK, dtype=jnp.int32)[None]
    packed = jnp.where(
        place < (n_block - x) * BLOCK,
        jnp.pad(upper_x, ((0, 0), (0, BLOCK))),
        jnp.pad(both[32:], ((0, 0), (BLOCK, 0))),
    )
    pieces = lax.all_to_all(packed.reshape(32, 9, BLOCK), ("z", "yh"), 0, 0, tiled=True)
    total = jnp.sum(pieces, axis=0)
    gathered = gather(total, ("z", "yh"))
    gathered = gather(gathered, ("x", "yl"))
    facing = swap(gathered)
    quarters = jnp.where(
        c == 0,
        jnp.stack([gathered, facing], axis=1),
        jnp.stack([facing, gathered], axis=1),
    )
    corner = quarters.reshape(n_block // 2, BLOCK, PANEL + BLOCK)
    right, inverse = factor(corner)

    gram = over_frames(lifted[:n_rows], masked)
    cross = over_frames(lifted[LAG:], masked)
    gram = lax.all_to_all(gram.reshape(n_z, n_yh * width, PANEL), "z", 0, 0, tiled=True)
    gram = jnp.sum(gram, axis=0).reshape(n_yh, width, PANEL)
    cross = cross.reshape(n_z, n_yh, width, PANEL).transpose(1, 0, 2, 3)
    cross = lax.all_to_all(cross.reshape(n_yh, n_z * width, PANEL), "yh", 0, 0, tiled=True)
    cross = jnp.sum(cross, axis=0).reshape(n_z, width, PANEL)
    gram = jnp.sum(lax.all_to_all(gram, "yh", 0, 0, tiled=True), axis=0) * F32(1.0 / FRAMES)
    cross = jnp.sum(lax.all_to_all(cross, "z", 0, 0, tiled=True), axis=0) * F32(1.0 / FRAMES)
    row_ids = tile * block + tm * width + jnp.arange(width, dtype=jnp.int32)[:, None]
    col_ids = jnp.arange(PANEL, dtype=jnp.int32)[None, :]
    gram = gram + jnp.where(row_ids == col_ids, F32(RIDGE), F32(0.0))

    solved = solve(jnp.concatenate([gram, cross], axis=0), right, inverse)
    return solved[:width], (solved[width:] * jnp.sqrt(F32(FRAMES))).T


def solution(mesh):
    fine = Mesh(mesh.devices.reshape(8, 4, 2, 4, 2), ("z", "yh", "c", "x", "yl"))
    tm, tile = ("z", "yh", "c"), ("x", "yl")
    return jax.shard_map(
        per_device,
        mesh=fine,
        in_specs=(P(tm, None), P(None, tile), P(tile), P(tm)),
        out_specs=(P(tile + tm, None), P(None, tile + tm)),
        check_vma=False,
    )
```

```python
import jax
import jax.numpy as jnp
from jax import lax
from jax.experimental import pallas as pl
from jax.experimental.pallas import tpu as pltpu
from jax.sharding import Mesh, PartitionSpec as P

PANEL = 1024
LAG = 96
BLOCK = 128
GROUP = 16
RIDGE = 0.05
FRAMES = 32768

F32 = jnp.float32
BF16 = jnp.bfloat16

COSINE = (
    1.0,
    -19.73920440673828,
    64.93911743164062,
    -85.45016479492188,
    60.16783142089844,
    -25.968313217163086,
    6.529610633850098,
)


def cosine(angle):
    turns = angle * F32(0.15915494309189535)
    turns = turns - jnp.round(turns)
    square = turns * turns
    value = jnp.full_like(square, COSINE[-1])
    for factor in COSINE[-2::-1]:
        value = value * square + F32(factor)
    return value


def lift_rows(rows, freq, phase):
    angle = jnp.dot(rows, freq, preferred_element_type=F32) + phase.astype(F32)
    return cosine(angle).astype(BF16)


def over_frames(left, right):
    return lax.dot_general(left, right, (((0,), (0,)), ((), ())), preferred_element_type=F32)


def swap(value):
    return lax.ppermute(value, "c", [(0, 1), (1, 0)])


def gather(value, axes):
    count = 1
    for axis in axes:
        count *= lax.axis_size(axis)
    copies = jnp.broadcast_to(value[None], (count,) + value.shape)
    return lax.all_to_all(copies, axes, 0, 0, tiled=True)


def product(left, right, dims=((1,), (0,))):
    return lax.dot_general(
        left, right, (dims, ((), ())), precision=lax.Precision.HIGHEST, preferred_element_type=F32
    )


def inverse_factor(block):
    row = lax.broadcasted_iota(jnp.int32, (BLOCK, BLOCK), 0)
    col = lax.broadcasted_iota(jnp.int32, (BLOCK, BLOCK), 1)
    eye = (row == col).astype(F32)
    rows = lax.broadcasted_iota(jnp.int32, (GROUP, BLOCK), 0)
    left, right = [], []
    s, t = block[:GROUP], eye[:GROUP]
    for lo in range(0, BLOCK, GROUP):
        mid, hi = lo + GROUP, lo + 2 * GROUP
        more = mid < BLOCK
        cols = [jnp.broadcast_to(s[:, lo + k : lo + k + 1], (GROUP, BLOCK)) for k in range(GROUP)]
        if more:
            below, beside = block[mid:hi], eye[mid:hi]
            if lo:
                above = jnp.concatenate(left, axis=0)
                both = jnp.concatenate([above, jnp.concatenate(right, axis=0)], axis=1)
                done = product(above[:, mid:hi], both, ((0,), (0,)))
                below, beside = below - done[:, :BLOCK], beside - done[:, BLOCK:]
            low = [
                jnp.broadcast_to(below[:, lo + k : lo + k + 1], (GROUP, BLOCK))
                for k in range(GROUP)
            ]
        diag = jnp.ones((GROUP, BLOCK), F32)
        for j in range(GROUP):
            pivot = cols[j][j : j + 1]
            diag = jnp.where(rows == j, pivot, diag)
            over = pltpu.reciprocal(pivot, approx=True)
            if j < GROUP - 1:
                ratio = jnp.where(rows > j, cols[j] * over, 0.0)
                for k in range(j + 1, GROUP):
                    cols[k] = cols[k] - ratio * cols[k][j : j + 1]
                s, t = s - ratio * s[j : j + 1], t - ratio * t[j : j + 1]
            if more:
                ratio = low[j] * over
                for k in range(j + 1, GROUP):
                    low[k] = low[k] - ratio * cols[k][j : j + 1]
                below, beside = below - ratio * s[j : j + 1], beside - ratio * t[j : j + 1]
        scale = lax.rsqrt(diag)
        left.append(s * scale)
        right.append(t * scale)
        if more:
            s, t = below, beside
    return jnp.concatenate(right, axis=0)


def factor_kernel(place_ref, mine_ref, facing_ref, next_ref, inverse_ref, a_ref):
    blocks = PANEL // BLOCK
    core, yl = place_ref[0], place_ref[1]
    for ref, cc in ((mine_ref, core), (facing_ref, 1 - core)):
        for side, yy in ((0, yl), (1, 1 - yl)):
            for x in range(blocks // 2):
                for tile in range(36):
                    group, j = tile // 9, tile % 9
                    i, col = (x, x + j) if j < blocks - x else (blocks - 1 - x, j - 1)
                    start = pl.multiple_of(i * BLOCK + yy * 64 + cc * 32 + group * 8, 8)
                    a_ref[pl.ds(start, 8), col * BLOCK : (col + 1) * BLOCK] = ref[
                        side, tile // 5, x, tile % 5
                    ] * F32(1.0 / FRAMES)
    row = lax.broadcasted_iota(jnp.int32, (BLOCK, BLOCK), 0)
    col = lax.broadcasted_iota(jnp.int32, (BLOCK, BLOCK), 1)
    ridge = jnp.where(row == col, F32(RIDGE), F32(0.0))
    for i in range(blocks):
        lo = i * BLOCK
        a_ref[lo : lo + BLOCK, lo : lo + BLOCK] = a_ref[lo : lo + BLOCK, lo : lo + BLOCK] + ridge
    for p in range(blocks):
        lo = p * BLOCK
        hi = lo + BLOCK
        inverse = inverse_factor(a_ref[lo:hi, lo:hi])
        inverse_ref[p] = inverse
        if p + 1 < blocks:
            upper = product(inverse, a_ref[lo:hi, hi:])
            for k in range(hi, PANEL, BLOCK):
                a_ref[k : k + BLOCK, k:] = a_ref[k : k + BLOCK, k:] - product(
                    upper[:, k - hi : k - hi + BLOCK], upper[:, k - hi :], ((0,), (0,))
                )
            next_ref[lo:hi, hi:] = product(inverse, upper, ((0,), (0,)))


def factor(place, mine, facing):
    out = jax.ShapeDtypeStruct
    in_vmem = pl.BlockSpec(memory_space=pltpu.VMEM)
    return pl.pallas_call(
        factor_kernel,
        out_shape=(
            out((PANEL, PANEL), F32),
            out((PANEL // BLOCK, BLOCK, BLOCK), F32),
        ),
        in_specs=[pl.BlockSpec(memory_space=pltpu.SMEM), in_vmem, in_vmem],
        out_specs=(in_vmem, in_vmem),
        scratch_shapes=[pltpu.VMEM((PANEL, PANEL), F32)],
        compiler_params=pltpu.CompilerParams(vmem_limit_bytes=40 << 20),
        cost_estimate=pl.CostEstimate(
            flops=2_000_000_000, bytes_accessed=10_000_000, transcendentals=0
        ),
        name="factor",
    )(place, mine, facing)


def solve_kernel(first_ref, parts_ref, next_ref, inverse_ref, out_ref):
    rest = parts_ref[0]
    for k in range(1, parts_ref.shape[0]):
        rest = rest + parts_ref[k]
    row = lax.broadcasted_iota(jnp.int32, rest.shape, 0)
    col = lax.broadcasted_iota(jnp.int32, rest.shape, 1)
    on_diagonal = jnp.logical_and(row < rest.shape[0] // 2, row + first_ref[0] == col)
    rest = rest * F32(1.0 / FRAMES) + jnp.where(on_diagonal, F32(RIDGE), F32(0.0))
    for p in range(PANEL // BLOCK):
        lo = p * BLOCK
        head = rest[:, :BLOCK]
        out_ref[:, lo : lo + BLOCK] = product(head, inverse_ref[p], ((1,), (1,)))
        if lo + BLOCK < PANEL:
            rest = rest[:, BLOCK:] - product(head, next_ref[lo : lo + BLOCK, lo + BLOCK :])


def solve(first_row, parts, right, inverse):
    in_vmem = pl.BlockSpec(memory_space=pltpu.VMEM)
    return pl.pallas_call(
        solve_kernel,
        out_shape=jax.ShapeDtypeStruct(parts.shape[1:], F32),
        in_specs=[pl.BlockSpec(memory_space=pltpu.SMEM)] + [in_vmem] * 3,
        out_specs=in_vmem,
        compiler_params=pltpu.CompilerParams(vmem_limit_bytes=40 << 20),
        cost_estimate=pl.CostEstimate(
            flops=4_000_000_000, bytes_accessed=5_000_000, transcendentals=0
        ),
        name="solve",
    )(first_row, parts, right, inverse)


def per_device(frames, freq, phase, seg_end):
    n_z, n_c = lax.axis_size("z"), lax.axis_size("c")
    n_yh = lax.axis_size("yhh") * lax.axis_size("yhl")
    n_y = n_yh * lax.axis_size("yl")
    n_tm = n_z * n_yh * n_c
    f_dev, din = frames.shape
    block = freq.shape[1]
    width = block // n_tm
    c = lax.axis_index("c")
    yh = lax.axis_index("yhh") * lax.axis_size("yhl") + lax.axis_index("yhl")
    x = lax.axis_index("x")
    yl = lax.axis_index("yl")
    tm = (lax.axis_index("z") * n_yh + yh) * n_c + c
    tile = x * lax.axis_size("yl") + yl

    half = din // n_c
    mine = lax.dynamic_slice(freq, (c * half, 0), (half, block))
    chunks = jnp.concatenate(
        [mine.reshape(8, half // 8, block), jnp.broadcast_to(phase[None, None], (8, 1, block))],
        axis=1,
    )
    chunk = lax.all_to_all(chunks, ("x", "yl"), 0, 0, tiled=True)[0]

    halves = gather(chunk, ("x", "yl"))
    panel_phase = halves[0, half // 8]
    mine = halves[:, : half // 8].reshape(half, block)
    other = swap(mine)
    panel_freq = jnp.where(
        c == 0, jnp.concatenate([mine, other]), jnp.concatenate([other, mine])
    )

    where_at = tm * f_dev + jnp.arange(f_dev, dtype=jnp.int32)
    valid = (where_at + LAG <= seg_end).astype(BF16)
    head = lax.ppermute(
        frames[:LAG],
        ("z", "yhh", "yhl", "c"),
        [(source, source - 1) for source in range(1, n_tm)],
    )
    near = jnp.concatenate([frames, valid.reshape(f_dev // din, din), head], axis=0)
    near_other = swap(near)

    def chip_rows(own, others):
        first = jnp.where(c == 0, own, others)
        second = jnp.where(c == 0, others, own)
        rows = jnp.concatenate([first[:f_dev], second[:f_dev], second[f_dev + 1 :]])
        return rows, jnp.concatenate([first[f_dev], second[f_dev]])[:, None]

    n_rows = n_c * f_dev
    rows, both_valid = chip_rows(near, near_other)
    panel = lift_rows(rows[:n_rows], panel_freq, panel_phase)
    masked = panel * both_valid
    quarter = yl * n_c + c
    n_block = PANEL // BLOCK
    rows_x = lax.dynamic_slice(panel, (0, x * BLOCK + quarter * 32), (n_rows, 32))
    rows_y = lax.dynamic_slice(panel, (0, (n_block - 1 - x) * BLOCK + quarter * 32), (n_rows, 32))
    both = over_frames(jnp.concatenate([rows_x, rows_y], axis=1), masked)
    padded = jnp.pad(both[:32], ((0, 0), (0, BLOCK * n_block // 2)))
    upper_x = lax.dynamic_slice(padded, (0, x * BLOCK), (32, PANEL))
    place = jnp.arange(PANEL + BLOCK, dtype=jnp.int32)[None]
    packed = jnp.where(
        place < (n_block - x) * BLOCK,
        jnp.pad(upper_x, ((0, 0), (0, BLOCK))),
        jnp.pad(both[32:], ((0, 0), (BLOCK, 0))),
    )
    packed = packed.reshape(4, 8, 9, BLOCK).transpose(0, 2, 1, 3).reshape(36, 8, BLOCK)
    packed = jnp.pad(packed, ((0, 4), (0, 0), (0, 0))).reshape(8, 5, 8, BLOCK)
    route = [(y, (y + 1) % n_y if y % 2 else (y - 1) % n_y) for y in range(n_y)]
    near, packed = lax.optimization_barrier((near, packed))
    far = lax.ppermute(near, ("yhh", "yhl", "yl"), route)
    total = jnp.sum(lax.all_to_all(packed, "z", 0, 0, tiled=True), axis=0)
    far, total = lax.optimization_barrier((far, total))
    far_other = swap(far)
    total = jnp.sum(gather(total, ("yhh", "yhl")), axis=0)
    far_other, total = lax.optimization_barrier((far_other, total))
    gathered = gather(total, ("z", "x")).reshape(n_z, n_block // 2, 5, 8, BLOCK)

    n_own = block // (2 * n_c)
    column = jnp.arange(n_own, dtype=jnp.int32)
    z_of, yh_of = column // (2 * width), 2 * ((column // width) % 2) + yh % 2
    source = ((z_of * n_yh + yh_of) * n_c + c) * width + column % width
    pick = (jnp.arange(block, dtype=jnp.int32)[:, None] == source[None, :]).astype(BF16)
    own_freq = jnp.dot(freq, pick, preferred_element_type=F32).astype(BF16)
    own_phase = jnp.dot(phase[None], pick, preferred_element_type=F32)[0]

    def over_chip(chip, panel_rows):
        lifted = lift_rows(chip, own_freq, own_phase)
        pairs = jnp.concatenate([lifted[:n_rows], lifted[LAG:]], axis=1)
        return over_frames(pairs, panel_rows)

    far_rows, far_valid = chip_rows(far, far_other)
    far_panel = lift_rows(far_rows[:n_rows], panel_freq, panel_phase) * far_valid
    parts = over_chip(rows, masked) + over_chip(far_rows, far_panel)
    parts = parts.reshape(2, n_z, 2, width, PANEL).transpose(1, 2, 0, 3, 4)
    parts, gathered = lax.optimization_barrier((parts, gathered))
    parts = lax.all_to_all(
        parts.reshape(n_z * 2, 2 * width, PANEL), ("z", "yhh"), 0, 0, tiled=True
    )

    beside = lax.ppermute(gathered[: n_z // 2], "yl", [(0, 1), (1, 0)])
    across = lax.ppermute(gathered[n_z // 2 :], ("yhh", "yhl", "yl"), route)
    both = jnp.stack([gathered, jnp.concatenate([beside, across], axis=0)])
    right, inverse = factor(jnp.stack([c, yl]), both, swap(both))
    parts, inverse = lax.optimization_barrier((parts, inverse))
    first_row = (tile * block + tm * width).astype(jnp.int32).reshape(1)
    solved = solve(first_row, parts, right, inverse)
    return solved[:width], (solved[width:] * jnp.sqrt(F32(FRAMES))).T


def solution(mesh):
    fine = Mesh(mesh.devices.reshape(8, 2, 2, 2, 4, 2), ("z", "yhh", "yhl", "c", "x", "yl"))
    tm, tile = ("z", "yhh", "yhl", "c"), ("x", "yl")
    return jax.shard_map(
        per_device,
        mesh=fine,
        in_specs=(P(tm, None), P(None, tile), P(tile), P(tm)),
        out_specs=(P(tile + tm, None), P(None, tile + tm)),
        check_vma=False,
    )
```

```python
import jax
import jax.numpy as jnp
from jax import lax
from jax.experimental import pallas as pl
from jax.experimental.pallas import tpu as pltpu
from jax.sharding import Mesh, PartitionSpec as P

PANEL = 1024
LAG = 96
BLOCK = 128
GROUP = 16
RIDGE = 0.05
FRAMES = 32768

F32 = jnp.float32
BF16 = jnp.bfloat16

COSINE = (
    1.0,
    -19.73920440673828,
    64.93911743164062,
    -85.45016479492188,
    60.16783142089844,
    -25.968313217163086,
    6.529610633850098,
)


def cosine(angle):
    turns = angle * F32(0.15915494309189535)
    turns = turns - jnp.round(turns)
    square = turns * turns
    value = jnp.full_like(square, COSINE[-1])
    for factor in COSINE[-2::-1]:
        value = value * square + F32(factor)
    return value


def lift_rows(rows, freq, phase):
    angle = jnp.dot(rows, freq, preferred_element_type=F32) + phase.astype(F32)
    return cosine(angle).astype(BF16)


def over_frames(left, right):
    return lax.dot_general(left, right, (((0,), (0,)), ((), ())), preferred_element_type=F32)


def swap(value):
    return lax.ppermute(value, "c", [(0, 1), (1, 0)])


def gather(value, axes):
    count = 1
    for axis in axes:
        count *= lax.axis_size(axis)
    copies = jnp.broadcast_to(value[None], (count,) + value.shape)
    return lax.all_to_all(copies, axes, 0, 0, tiled=True)


def product(left, right, dims=((1,), (0,))):
    return lax.dot_general(
        left, right, (dims, ((), ())), precision=lax.Precision.HIGHEST, preferred_element_type=F32
    )


def inverse_factor(block):
    row = lax.broadcasted_iota(jnp.int32, (BLOCK, BLOCK), 0)
    col = lax.broadcasted_iota(jnp.int32, (BLOCK, BLOCK), 1)
    eye = (row == col).astype(F32)
    rows = lax.broadcasted_iota(jnp.int32, (GROUP, BLOCK), 0)
    left, right = [], []
    s, t = block[:GROUP], eye[:GROUP]
    for lo in range(0, BLOCK, GROUP):
        mid, hi = lo + GROUP, lo + 2 * GROUP
        more = mid < BLOCK
        cols = [jnp.broadcast_to(s[:, lo + k : lo + k + 1], (GROUP, BLOCK)) for k in range(GROUP)]
        if more:
            below, beside = block[mid:hi], eye[mid:hi]
            if lo:
                above = jnp.concatenate(left, axis=0)
                both = jnp.concatenate([above, jnp.concatenate(right, axis=0)], axis=1)
                done = product(above[:, mid:hi], both, ((0,), (0,)))
                below, beside = below - done[:, :BLOCK], beside - done[:, BLOCK:]
            low = [
                jnp.broadcast_to(below[:, lo + k : lo + k + 1], (GROUP, BLOCK))
                for k in range(GROUP)
            ]
        diag = jnp.ones((GROUP, BLOCK), F32)
        for j in range(GROUP):
            pivot = cols[j][j : j + 1]
            diag = jnp.where(rows == j, pivot, diag)
            over = pltpu.reciprocal(pivot, approx=True)
            if j < GROUP - 1:
                ratio = jnp.where(rows > j, cols[j] * over, 0.0)
                for k in range(j + 1, GROUP):
                    cols[k] = cols[k] - ratio * cols[k][j : j + 1]
                s, t = s - ratio * s[j : j + 1], t - ratio * t[j : j + 1]
            if more:
                ratio = low[j] * over
                for k in range(j + 1, GROUP):
                    low[k] = low[k] - ratio * cols[k][j : j + 1]
                below, beside = below - ratio * s[j : j + 1], beside - ratio * t[j : j + 1]
        scale = lax.rsqrt(diag)
        left.append(s * scale)
        right.append(t * scale)
        if more:
            s, t = below, beside
    return jnp.concatenate(right, axis=0)


def next_place(p):
    last = PANEL // BLOCK - 1
    width = (last - p) * BLOCK
    return (p * BLOCK, 0, width) if p <= last // 2 else ((last - p) * BLOCK, p * BLOCK, width)


def factor_kernel(core_ref, mine_ref, facing_ref, next_ref, inverse_ref, a_ref):
    blocks = PANEL // BLOCK
    core = core_ref[0]
    for ref, cc in ((mine_ref, core), (facing_ref, 1 - core)):
        for k in range(blocks):
            x, yl = k // 2, k % 2
            for tile in range(36):
                group, j = tile // 9, tile % 9
                i, col = (x, x + j) if j < blocks - x else (blocks - 1 - x, j - 1)
                start = pl.multiple_of(i * BLOCK + yl * 64 + group * 8 + cc * 32, 8)
                a_ref[pl.ds(start, 8), col * BLOCK : (col + 1) * BLOCK] = ref[k, tile] * F32(
                    1.0 / FRAMES
                )
    row = lax.broadcasted_iota(jnp.int32, (BLOCK, BLOCK), 0)
    col = lax.broadcasted_iota(jnp.int32, (BLOCK, BLOCK), 1)
    ridge = jnp.where(row == col, F32(RIDGE), F32(0.0))
    for i in range(blocks):
        lo = i * BLOCK
        a_ref[lo : lo + BLOCK, lo : lo + BLOCK] = a_ref[lo : lo + BLOCK, lo : lo + BLOCK] + ridge
    for p in range(blocks):
        lo = p * BLOCK
        hi = lo + BLOCK
        inverse = inverse_factor(a_ref[lo:hi, lo:hi])
        inverse_ref[p] = inverse
        if p + 1 < blocks:
            upper = product(inverse, a_ref[lo:hi, hi:])
            for k in range(hi, PANEL, BLOCK):
                a_ref[k : k + BLOCK, k:] = a_ref[k : k + BLOCK, k:] - product(
                    upper[:, k - hi : k - hi + BLOCK], upper[:, k - hi :], ((0,), (0,))
                )
            top, start, width = next_place(p)
            next_ref[top : top + BLOCK, start : start + width] = product(
                inverse, upper, ((0,), (0,))
            )


def factor(core, mine, facing):
    out = jax.ShapeDtypeStruct
    in_vmem = pl.BlockSpec(memory_space=pltpu.VMEM)
    return pl.pallas_call(
        factor_kernel,
        out_shape=(
            out((PANEL // 2, PANEL - BLOCK), F32),
            out((PANEL // BLOCK, BLOCK, BLOCK), F32),
        ),
        in_specs=[pl.BlockSpec(memory_space=pltpu.SMEM), in_vmem, in_vmem],
        out_specs=(in_vmem, in_vmem),
        scratch_shapes=[pltpu.VMEM((PANEL, PANEL), F32)],
        compiler_params=pltpu.CompilerParams(vmem_limit_bytes=16 << 20),
        cost_estimate=pl.CostEstimate(
            flops=45_000_000_000, bytes_accessed=10_000_000, transcendentals=0
        ),
        name="factor",
    )(core, mine, facing)


def solve_kernel(first_ref, parts_ref, next_ref, inverse_ref, out_ref):
    rest = parts_ref[0]
    for k in range(1, parts_ref.shape[0]):
        rest = rest + parts_ref[k]
    row = lax.broadcasted_iota(jnp.int32, rest.shape, 0)
    col = lax.broadcasted_iota(jnp.int32, rest.shape, 1)
    on_diagonal = jnp.logical_and(row < rest.shape[0] // 2, row + first_ref[0] == col)
    rest = rest * F32(1.0 / FRAMES) + jnp.where(on_diagonal, F32(RIDGE), F32(0.0))
    for p in range(PANEL // BLOCK):
        lo = p * BLOCK
        head = rest[:, :BLOCK]
        out_ref[:, lo : lo + BLOCK] = product(head, inverse_ref[p], ((1,), (1,)))
        if lo + BLOCK < PANEL:
            top, start, width = next_place(p)
            rest = rest[:, BLOCK:] - product(
                head, next_ref[top : top + BLOCK, start : start + width]
            )


def solve(first_row, parts, right, inverse):
    in_vmem = pl.BlockSpec(memory_space=pltpu.VMEM)
    return pl.pallas_call(
        solve_kernel,
        out_shape=jax.ShapeDtypeStruct(parts.shape[1:], F32),
        in_specs=[pl.BlockSpec(memory_space=pltpu.SMEM)] + [in_vmem] * 3,
        out_specs=in_vmem,
        compiler_params=pltpu.CompilerParams(vmem_limit_bytes=8 << 20),
        cost_estimate=pl.CostEstimate(
            flops=4_000_000_000, bytes_accessed=5_000_000, transcendentals=0
        ),
        name="solve",
    )(first_row, parts, right, inverse)


def per_device(frames, freq, phase, seg_end):
    n_z, n_c = lax.axis_size("z"), lax.axis_size("c")
    n_yh = lax.axis_size("yhh") * lax.axis_size("yhl")
    n_y = n_yh * lax.axis_size("yl")
    n_tm = n_z * n_yh * n_c
    f_dev, din = frames.shape
    block = freq.shape[1]
    width = block // n_tm
    c = lax.axis_index("c")
    yh = lax.axis_index("yhh") * lax.axis_size("yhl") + lax.axis_index("yhl")
    x = lax.axis_index("x")
    yl = lax.axis_index("yl")
    tm = (lax.axis_index("z") * n_yh + yh) * n_c + c
    tile = x * lax.axis_size("yl") + yl

    half = din // n_c
    mine = lax.dynamic_slice(freq, (c * half, 0), (half, block))
    chunks = jnp.concatenate(
        [mine.reshape(8, half // 8, block), jnp.broadcast_to(phase[None, None], (8, 1, block))],
        axis=1,
    )
    chunk = lax.all_to_all(chunks, ("x", "yl"), 0, 0, tiled=True)[0]

    halves = gather(chunk, ("x", "yl"))
    panel_phase = halves[0, half // 8]
    mine = halves[:, : half // 8].reshape(half, block)
    other = swap(mine)
    panel_freq = jnp.where(
        c == 0, jnp.concatenate([mine, other]), jnp.concatenate([other, mine])
    )

    where_at = tm * f_dev + jnp.arange(f_dev, dtype=jnp.int32)
    valid = (where_at + LAG <= seg_end).astype(BF16)
    head = lax.ppermute(
        frames[:LAG],
        ("z", "yhh", "yhl", "c"),
        [(source, source - 1) for source in range(1, n_tm)],
    )
    near = jnp.concatenate([frames, valid.reshape(f_dev // din, din), head], axis=0)
    near_other = swap(near)

    def chip_rows(own, others):
        first = jnp.where(c == 0, own, others)
        second = jnp.where(c == 0, others, own)
        rows = jnp.concatenate([first[:f_dev], second[:f_dev], second[f_dev + 1 :]])
        return rows, jnp.concatenate([first[f_dev], second[f_dev]])[:, None]

    n_rows = n_c * f_dev
    rows, both_valid = chip_rows(near, near_other)
    panel = lift_rows(rows[:n_rows], panel_freq, panel_phase)
    masked = panel * both_valid
    quarter = yl * n_c + c
    n_block = PANEL // BLOCK
    rows_x = lax.dynamic_slice(panel, (0, x * BLOCK + quarter * 32), (n_rows, 32))
    rows_y = lax.dynamic_slice(panel, (0, (n_block - 1 - x) * BLOCK + quarter * 32), (n_rows, 32))
    both = over_frames(jnp.concatenate([rows_x, rows_y], axis=1), masked)
    padded = jnp.pad(both[:32], ((0, 0), (0, BLOCK * n_block // 2)))
    upper_x = lax.dynamic_slice(padded, (0, x * BLOCK), (32, PANEL))
    place = jnp.arange(PANEL + BLOCK, dtype=jnp.int32)[None]
    packed = jnp.where(
        place < (n_block - x) * BLOCK,
        jnp.pad(upper_x, ((0, 0), (0, BLOCK))),
        jnp.pad(both[32:], ((0, 0), (BLOCK, 0))),
    )
    packed = packed.reshape(4, 8, 9, BLOCK).transpose(0, 2, 1, 3).reshape(36, 8, BLOCK)
    packed = jnp.pad(packed, ((0, 4), (0, 0), (0, 0))).reshape(8, 5, 8, BLOCK)
    route = [(y, (y + 1) % n_y if y % 2 else (y - 1) % n_y) for y in range(n_y)]
    near, packed = lax.optimization_barrier((near, packed))
    far = lax.ppermute(near, ("yhh", "yhl", "yl"), route)
    total = jnp.sum(lax.all_to_all(packed, "z", 0, 0, tiled=True), axis=0)
    far, total = lax.optimization_barrier((far, total))
    far_other = swap(far)
    total = jnp.sum(gather(total, ("yhh", "yhl")), axis=0)
    far_other, total = lax.optimization_barrier((far_other, total))
    gathered = gather(gather(total, ("z",)).reshape(40, 8, BLOCK), ("x", "yl"))

    n_own = block // (2 * n_c)
    column = jnp.arange(n_own, dtype=jnp.int32)
    z_of, yh_of = column // (2 * width), 2 * ((column // width) % 2) + yh % 2
    source = ((z_of * n_yh + yh_of) * n_c + c) * width + column % width
    pick = (jnp.arange(block, dtype=jnp.int32)[:, None] == source[None, :]).astype(BF16)
    own_freq = jnp.dot(freq, pick, preferred_element_type=F32).astype(BF16)
    own_phase = jnp.dot(phase[None], pick, preferred_element_type=F32)[0]

    def over_chip(chip, panel_rows):
        lifted = lift_rows(chip, own_freq, own_phase)
        pairs = jnp.concatenate([lifted[:n_rows], lifted[LAG:]], axis=1)
        return over_frames(pairs, panel_rows)

    far_rows, far_valid = chip_rows(far, far_other)
    far_panel = lift_rows(far_rows[:n_rows], panel_freq, panel_phase) * far_valid
    parts = over_chip(rows, masked) + over_chip(far_rows, far_panel)
    parts = parts.reshape(2, n_z, 2, width, PANEL).transpose(1, 2, 0, 3, 4)
    parts, gathered = lax.optimization_barrier((parts, gathered))
    right, inverse = factor(c.reshape(1), gathered, swap(gathered))
    parts = lax.all_to_all(
        parts.reshape(n_z * 2, 2 * width, PANEL), ("z", "yhh"), 0, 0, tiled=True
    )
    first_row = (tile * block + tm * width).astype(jnp.int32).reshape(1)
    solved = solve(first_row, parts, right, inverse)
    return solved[:width], (solved[width:] * jnp.sqrt(F32(FRAMES))).T


def solution(mesh):
    fine = Mesh(mesh.devices.reshape(8, 2, 2, 2, 4, 2), ("z", "yhh", "yhl", "c", "x", "yl"))
    tm, tile = ("z", "yhh", "yhl", "c"), ("x", "yl")
    return jax.shard_map(
        per_device,
        mesh=fine,
        in_specs=(P(tm, None), P(None, tile), P(tile), P(tm)),
        out_specs=(P(tile + tm, None), P(None, tile + tm)),
        check_vma=False,
    )
```

```python
import jax
import jax.numpy as jnp
from jax import lax
from jax.experimental import pallas as pl
from jax.experimental.pallas import tpu as pltpu
from jax.sharding import Mesh, PartitionSpec as P

PANEL = 1024
LAG = 96
BLOCK = 128
GROUP = 16
RIDGE = 0.05
FRAMES = 32768

F32 = jnp.float32
BF16 = jnp.bfloat16

COSINE = (
    1.0,
    -19.73920440673828,
    64.93911743164062,
    -85.45016479492188,
    60.16783142089844,
    -25.968313217163086,
    6.529610633850098,
)


def cosine(angle):
    turns = angle * F32(0.15915494309189535)
    turns = turns - jnp.round(turns)
    square = turns * turns
    value = jnp.full_like(square, COSINE[-1])
    for factor in COSINE[-2::-1]:
        value = value * square + F32(factor)
    return value


def lift_rows(rows, freq, phase):
    angle = jnp.dot(rows, freq, preferred_element_type=F32) + phase.astype(F32)
    return cosine(angle).astype(BF16)


def over_frames(left, right):
    return lax.dot_general(left, right, (((0,), (0,)), ((), ())), preferred_element_type=F32)


def swap(value):
    return lax.ppermute(value, "c", [(0, 1), (1, 0)])


def gather(value, axes):
    count = 1
    for axis in axes:
        count *= lax.axis_size(axis)
    copies = jnp.broadcast_to(value[None], (count,) + value.shape)
    return lax.all_to_all(copies, axes, 0, 0, tiled=True)


def product(left, right, dims=((1,), (0,))):
    return lax.dot_general(
        left, right, (dims, ((), ())), precision=lax.Precision.HIGHEST, preferred_element_type=F32
    )


def inverse_factor(block):
    row = lax.broadcasted_iota(jnp.int32, (BLOCK, BLOCK), 0)
    col = lax.broadcasted_iota(jnp.int32, (BLOCK, BLOCK), 1)
    eye = (row == col).astype(F32)
    rows = lax.broadcasted_iota(jnp.int32, (GROUP, BLOCK), 0)
    left, right = [], []
    s, t = block[:GROUP], eye[:GROUP]
    for lo in range(0, BLOCK, GROUP):
        mid, hi = lo + GROUP, lo + 2 * GROUP
        more = mid < BLOCK
        cols = [jnp.broadcast_to(s[:, lo + k : lo + k + 1], (GROUP, BLOCK)) for k in range(GROUP)]
        if more:
            below, beside = block[mid:hi], eye[mid:hi]
            if lo:
                above = jnp.concatenate(left, axis=0)
                both = jnp.concatenate([above, jnp.concatenate(right, axis=0)], axis=1)
                done = product(above[:, mid:hi], both, ((0,), (0,)))
                below, beside = below - done[:, :BLOCK], beside - done[:, BLOCK:]
            low = [
                jnp.broadcast_to(below[:, lo + k : lo + k + 1], (GROUP, BLOCK))
                for k in range(GROUP)
            ]
        diag = jnp.ones((GROUP, BLOCK), F32)
        for j in range(GROUP):
            pivot = cols[j][j : j + 1]
            diag = jnp.where(rows == j, pivot, diag)
            over = pltpu.reciprocal(pivot, approx=True)
            if j < GROUP - 1:
                ratio = jnp.where(rows > j, cols[j] * over, 0.0)
                for k in range(j + 1, GROUP):
                    cols[k] = cols[k] - ratio * cols[k][j : j + 1]
                s, t = s - ratio * s[j : j + 1], t - ratio * t[j : j + 1]
            if more:
                ratio = low[j] * over
                for k in range(j + 1, GROUP):
                    low[k] = low[k] - ratio * cols[k][j : j + 1]
                below, beside = below - ratio * s[j : j + 1], beside - ratio * t[j : j + 1]
        scale = lax.rsqrt(diag)
        left.append(s * scale)
        right.append(t * scale)
        if more:
            s, t = below, beside
    return jnp.concatenate(right, axis=0)


def next_place(p):
    last = PANEL // BLOCK - 1
    width = (last - p) * BLOCK
    return (p * BLOCK, 0, width) if p <= last // 2 else ((last - p) * BLOCK, p * BLOCK, width)


def factor_kernel(core_ref, mine_ref, facing_ref, next_ref, inverse_ref, a_ref):
    blocks = PANEL // BLOCK
    core = core_ref[0]
    for ref, cc in ((mine_ref, core), (facing_ref, 1 - core)):
        for k in range(blocks):
            x, yl = k // 2, k % 2
            for tile in range(36):
                group, j = tile // 9, tile % 9
                i, col = (x, x + j) if j < blocks - x else (blocks - 1 - x, j - 1)
                start = pl.multiple_of(i * BLOCK + yl * 64 + group * 8 + cc * 32, 8)
                a_ref[pl.ds(start, 8), col * BLOCK : (col + 1) * BLOCK] = ref[k, tile] * F32(
                    1.0 / FRAMES
                )
    row = lax.broadcasted_iota(jnp.int32, (BLOCK, BLOCK), 0)
    col = lax.broadcasted_iota(jnp.int32, (BLOCK, BLOCK), 1)
    ridge = jnp.where(row == col, F32(RIDGE), F32(0.0))
    for i in range(blocks):
        lo = i * BLOCK
        a_ref[lo : lo + BLOCK, lo : lo + BLOCK] = a_ref[lo : lo + BLOCK, lo : lo + BLOCK] + ridge
    for p in range(blocks):
        lo = p * BLOCK
        hi = lo + BLOCK
        inverse = inverse_factor(a_ref[lo:hi, lo:hi])
        inverse_ref[p] = inverse
        if p + 1 < blocks:
            upper = product(inverse, a_ref[lo:hi, hi:])
            for k in range(hi, PANEL, BLOCK):
                a_ref[k : k + BLOCK, k:] = a_ref[k : k + BLOCK, k:] - product(
                    upper[:, k - hi : k - hi + BLOCK], upper[:, k - hi :], ((0,), (0,))
                )
            top, start, width = next_place(p)
            next_ref[top : top + BLOCK, start : start + width] = product(
                inverse, upper, ((0,), (0,))
            )


def factor(core, mine, facing):
    out = jax.ShapeDtypeStruct
    in_vmem = pl.BlockSpec(memory_space=pltpu.VMEM)
    return pl.pallas_call(
        factor_kernel,
        out_shape=(
            out((PANEL // 2, PANEL - BLOCK), F32),
            out((PANEL // BLOCK, BLOCK, BLOCK), F32),
        ),
        in_specs=[pl.BlockSpec(memory_space=pltpu.SMEM), in_vmem, in_vmem],
        out_specs=(in_vmem, in_vmem),
        scratch_shapes=[pltpu.VMEM((PANEL, PANEL), F32)],
        compiler_params=pltpu.CompilerParams(vmem_limit_bytes=16 << 20),
        cost_estimate=pl.CostEstimate(
            flops=45_000_000_000, bytes_accessed=10_000_000, transcendentals=0
        ),
        name="factor",
    )(core, mine, facing)


def solve_kernel(first_ref, own_ref, sent_ref, next_ref, inverse_ref, out_ref):
    rest = own_ref[...] + sent_ref[...]
    row = lax.broadcasted_iota(jnp.int32, rest.shape, 0)
    col = lax.broadcasted_iota(jnp.int32, rest.shape, 1)
    on_diagonal = jnp.logical_and(row < rest.shape[0] // 2, row + first_ref[0] == col)
    rest = rest * F32(1.0 / FRAMES) + jnp.where(on_diagonal, F32(RIDGE), F32(0.0))
    for p in range(PANEL // BLOCK):
        lo = p * BLOCK
        head = rest[:, :BLOCK]
        out_ref[:, lo : lo + BLOCK] = product(head, inverse_ref[p], ((1,), (1,)))
        if lo + BLOCK < PANEL:
            top, start, width = next_place(p)
            rest = rest[:, BLOCK:] - product(
                head, next_ref[top : top + BLOCK, start : start + width]
            )


def solve(first_row, own, sent, right, inverse):
    in_vmem = pl.BlockSpec(memory_space=pltpu.VMEM)
    return pl.pallas_call(
        solve_kernel,
        out_shape=jax.ShapeDtypeStruct(own.shape, F32),
        in_specs=[pl.BlockSpec(memory_space=pltpu.SMEM)] + [in_vmem] * 4,
        out_specs=in_vmem,
        compiler_params=pltpu.CompilerParams(vmem_limit_bytes=8 << 20),
        cost_estimate=pl.CostEstimate(
            flops=4_000_000_000, bytes_accessed=5_000_000, transcendentals=0
        ),
        name="solve",
    )(first_row, own, sent, right, inverse)


def per_device(frames, freq, phase, seg_end):
    n_z, n_c = lax.axis_size("z"), lax.axis_size("c")
    n_yh = lax.axis_size("yhh") * lax.axis_size("yhl")
    n_y = n_yh * lax.axis_size("yl")
    n_tm = n_z * n_yh * n_c
    f_dev, din = frames.shape
    block = freq.shape[1]
    width = block // n_tm
    c = lax.axis_index("c")
    yh = lax.axis_index("yhh") * lax.axis_size("yhl") + lax.axis_index("yhl")
    x = lax.axis_index("x")
    yl = lax.axis_index("yl")
    tm = (lax.axis_index("z") * n_yh + yh) * n_c + c
    tile = x * lax.axis_size("yl") + yl

    half = din // n_c
    mine = lax.dynamic_slice(freq, (c * half, 0), (half, block))
    chunks = jnp.concatenate(
        [mine.reshape(8, half // 8, block), jnp.broadcast_to(phase[None, None], (8, 1, block))],
        axis=1,
    )
    chunk = lax.all_to_all(chunks, ("x", "yl"), 0, 0, tiled=True)[0]

    halves = gather(chunk, ("x", "yl"))
    panel_phase = halves[0, half // 8]
    mine = halves[:, : half // 8].reshape(half, block)
    other = swap(mine)
    panel_freq = jnp.where(
        c == 0, jnp.concatenate([mine, other]), jnp.concatenate([other, mine])
    )

    where_at = tm * f_dev + jnp.arange(f_dev, dtype=jnp.int32)
    valid = (where_at + LAG <= seg_end).astype(BF16)
    head = lax.ppermute(
        frames[:LAG],
        ("z", "yhh", "yhl", "c"),
        [(source, source - 1) for source in range(1, n_tm)],
    )
    near = jnp.concatenate([frames, valid.reshape(f_dev // din, din), head], axis=0)
    near_other = swap(near)

    def chip_rows(own, others):
        first = jnp.where(c == 0, own, others)
        second = jnp.where(c == 0, others, own)
        rows = jnp.concatenate([first[:f_dev], second[:f_dev], second[f_dev + 1 :]])
        return rows, jnp.concatenate([first[f_dev], second[f_dev]])[:, None]

    n_rows = n_c * f_dev
    rows, both_valid = chip_rows(near, near_other)
    panel = lift_rows(rows[:n_rows], panel_freq, panel_phase)
    masked = panel * both_valid
    quarter = yl * n_c + c
    n_block = PANEL // BLOCK
    rows_x = lax.dynamic_slice(panel, (0, x * BLOCK + quarter * 32), (n_rows, 32))
    rows_y = lax.dynamic_slice(panel, (0, (n_block - 1 - x) * BLOCK + quarter * 32), (n_rows, 32))
    both = over_frames(jnp.concatenate([rows_x, rows_y], axis=1), masked)
    padded = jnp.pad(both[:32], ((0, 0), (0, BLOCK * n_block // 2)))
    upper_x = lax.dynamic_slice(padded, (0, x * BLOCK), (32, PANEL))
    place = jnp.arange(PANEL + BLOCK, dtype=jnp.int32)[None]
    packed = jnp.where(
        place < (n_block - x) * BLOCK,
        jnp.pad(upper_x, ((0, 0), (0, BLOCK))),
        jnp.pad(both[32:], ((0, 0), (BLOCK, 0))),
    )
    packed = packed.reshape(4, 8, 9, BLOCK).transpose(0, 2, 1, 3).reshape(36, 8, BLOCK)
    packed = jnp.pad(packed, ((0, 4), (0, 0), (0, 0))).reshape(8, 5, 8, BLOCK)
    route = [(y, (y + 1) % n_y if y % 2 else (y - 1) % n_y) for y in range(n_y)]
    near, packed = lax.optimization_barrier((near, packed))
    far = lax.ppermute(near, ("yhh", "yhl", "yl"), route)
    total = jnp.sum(lax.all_to_all(packed, "z", 0, 0, tiled=True), axis=0)
    far, total = lax.optimization_barrier((far, total))
    far_other = swap(far)
    total = jnp.sum(gather(total, ("yhh", "yhl")), axis=0)
    far_other, total = lax.optimization_barrier((far_other, total))
    gathered = gather(gather(total, ("z",)).reshape(40, 8, BLOCK), ("x", "yl"))

    n_own = block // (2 * n_c)
    column = jnp.arange(n_own, dtype=jnp.int32)
    z_of, yh_of = column // (2 * width), 2 * ((column // width) % 2) + yh % 2
    source = ((z_of * n_yh + yh_of) * n_c + c) * width + column % width
    pick = (jnp.arange(block, dtype=jnp.int32)[:, None] == source[None, :]).astype(BF16)
    own_freq = jnp.dot(freq, pick, preferred_element_type=F32).astype(BF16)
    own_phase = jnp.dot(phase[None], pick, preferred_element_type=F32)[0]

    def over_chip(chip, panel_rows):
        lifted = lift_rows(chip, own_freq, own_phase)
        pairs = jnp.concatenate([lifted[:n_rows], lifted[LAG:]], axis=1)
        return over_frames(pairs, panel_rows)

    far_rows, far_valid = chip_rows(far, far_other)
    far_panel = lift_rows(far_rows[:n_rows], panel_freq, panel_phase) * far_valid
    parts = over_chip(rows, masked) + over_chip(far_rows, far_panel)
    parts = parts.reshape(2, n_z, 2, width, PANEL).transpose(1, 2, 0, 3, 4)
    parts, gathered = lax.optimization_barrier((parts, gathered))
    right, inverse = factor(c.reshape(1), gathered, swap(gathered))
    parts = lax.all_to_all(parts.reshape(n_z, 4 * width, PANEL), "z", 0, 0, tiled=True)
    parts, inverse = lax.optimization_barrier((parts, inverse))
    parts = jnp.sum(parts, axis=0).reshape(2, 2 * width, PANEL)
    own = jnp.where(yh < 2, parts[0], parts[1])
    away = jnp.where(yh < 2, parts[1], parts[0])
    sent = lax.ppermute(away, "yhh", [(0, 1), (1, 0)])
    first_row = (tile * block + tm * width).astype(jnp.int32).reshape(1)
    solved = solve(first_row, own, sent, right, inverse)
    return solved[:width], (solved[width:] * jnp.sqrt(F32(FRAMES))).T


def solution(mesh):
    fine = Mesh(mesh.devices.reshape(8, 2, 2, 2, 4, 2), ("z", "yhh", "yhl", "c", "x", "yl"))
    tm, tile = ("z", "yhh", "yhl", "c"), ("x", "yl")
    return jax.shard_map(
        per_device,
        mesh=fine,
        in_specs=(P(tm, None), P(None, tile), P(tile), P(tm)),
        out_specs=(P(tile + tm, None), P(None, tile + tm)),
        check_vma=False,
    )
```
